32 devices in a mesh: dp: 4 (over x, core), ctx: 8 (over z, y).
Axes of the slice: x: 2, y: 2, z: 4, core: 2. Of those that a mesh axis runs over, the one named last changes fastest.
Arguments:
- queries: bfloat16 [4, 1024, 4096], P('dp', 'ctx'), may hold values from -256 to 256
- keys: bfloat16 [4, 1024, 4096], P('dp', 'ctx'), may hold values from -4 to 4
- gate: bfloat16 [4, 1024, 4096], P('dp', 'ctx'), may hold values from -6 to 6
- values: bfloat16 [4, 1024, 4096], P('dp', 'ctx'), may hold values from -6 to 6
- grad_out: bfloat16 [4, 1024, 4096], P('dp', 'ctx'), may hold values from -3 to 3
- doc_start: int32 [4, 1024], P('dp', 'ctx'), may hold values from 0 to 1023, as said below
- filter_taps: float32 [128, 4096], replicated, may hold values from -0.5 to 0.5
Outputs:
- grad_queries: bfloat16 [4, 1024, 4096], P('dp', 'ctx')
- grad_keys: bfloat16 [4, 1024, 4096], P('dp', 'ctx')
- grad_gate: bfloat16 [4, 1024, 4096], P('dp', 'ctx')
- grad_values: bfloat16 [4, 1024, 4096], P('dp', 'ctx')
- grad_filter: float32 [128, 4096], replicated
The draws below stay inside these ranges and needn't reach their ends.
Inputs may be any that keep to these rules, and one draw needn't show every extreme that they name: `doc_start`: entry t of a sequence is the first position of the document that holds position t: it never exceeds t and never falls along the sequence; every document has at most 640 positions, and every sequence holds one of exactly 640 positions.
All inputs are finite; a program needn't handle non-finite values.
Results may differ from the reference program's by a relative error of at most 0.0087.
Values may be sent and summed in bfloat16 or wider, within the bound.
A program may use at most 192 MiB of HBM per device.

```python
import jax
import jax.numpy as jnp
from jax import lax

HEADS = 32
HEAD_DIM = 128
FILT = 128
TOK_DEV = 128
ATT_HOPS = 5
CHANNELS = 4096
SEQ = 1024
BATCH = 4


def query_key_pair(key):
    shape = (BATCH, SEQ, HEADS, HEAD_DIM)
    first_key = jax.random.fold_in(key, 101)
    second_key = jax.random.fold_in(key, 102)
    query_out = jnp.clip(jax.random.normal(first_key, shape, jnp.float32), -4.0, 4.0)
    key_out = jnp.clip(jax.random.normal(second_key, shape, jnp.float32), -4.0, 4.0)
    query_out = jnp.clip(query_out, -256.0, 256.0).reshape(BATCH, SEQ, CHANNELS)
    key_out = jnp.clip(key_out, -4.0, 4.0).reshape(BATCH, SEQ, CHANNELS)
    return (query_out.astype(jnp.bfloat16), key_out.astype(jnp.bfloat16))


def draw_queries(key, part):
    return query_key_pair(key)[0]


def draw_keys(key, part):
    return query_key_pair(key)[1]


def draw_doc_start(key, part):
    doc_count = SEQ // TOK_DEV + 2
    most_len = ATT_HOPS * TOK_DEV
    rest = jax.random.randint(jax.random.fold_in(key, 31), (BATCH, doc_count - 2), TOK_DEV, most_len + 1)
    first = jax.random.randint(jax.random.fold_in(key, 32), (BATCH, 1), 1, TOK_DEV)
    longest = jnp.full((BATCH, 1), most_len, jnp.int32)
    lengths = jnp.concatenate((first.astype(jnp.int32), longest, rest.astype(jnp.int32)), 1)
    starts = (jnp.cumsum(lengths, 1) - lengths).astype(jnp.int32)
    positions = jnp.arange(SEQ, dtype=jnp.int32)
    passed = starts[:, None, :] <= positions[None, :, None]
    return jnp.max(jnp.where(passed, starts[:, None, :], 0), -1).astype(jnp.int32)


def block_levels(key, extent, shards, smallest, high):
    factor_of, own = 1.0, jax.random.fold_in(key, 6)
    for axis_at, parts in shards:
        steps = jnp.exp(jax.random.uniform(jax.random.fold_in(own, axis_at), (parts,), jnp.float32, smallest / len(shards), high / len(shards)))
        factor_of = factor_of * jnp.repeat(steps, extent[axis_at] // parts).reshape([-1 if axis == axis_at else 1 for axis in range(len(extent))])
    return factor_of


def bell_draw(key, dims, deviation, reach, pieces=(), kind=jnp.bfloat16):
    drawn = jax.random.normal(key, dims, jnp.float32) * deviation
    if len(pieces) > 0:
        drawn = block_levels(key, dims, pieces, -0.22, 0.18) * drawn
    return jnp.clip(drawn, min=-reach, max=reach).astype(kind)


def setup_inputs(seed: int = 0) -> dict:
    arg_keys = jax.random.split(jax.random.key(seed), 8)
    queries = draw_queries(jax.random.fold_in(arg_keys[7], 71), 0)
    keys = draw_keys(jax.random.fold_in(arg_keys[7], 71), 0)
    gate = bell_draw(arg_keys[2], (BATCH, SEQ, CHANNELS), 1.0, 6.0, ((0, 4), (1, 8)))
    values = bell_draw(arg_keys[3], (BATCH, SEQ, CHANNELS), 1.0, 6.0, ((0, 4), (1, 8)))
    grad_out = bell_draw(arg_keys[4], (BATCH, SEQ, CHANNELS), 0.5, 3.0, ((0, 4), (1, 8)))
    doc_start = draw_doc_start(jax.random.fold_in(arg_keys[7], 71), 0)
    filter_taps = bell_draw(arg_keys[6], (FILT, CHANNELS), FILT ** -0.5, 0.5, (), jnp.float32)
    return dict(queries=queries, keys=keys, gate=gate, values=values, grad_out=grad_out, doc_start=doc_start, filter_taps=filter_taps)


def causal_filter(signal, filter_taps):
    rim_len = FILT - 1
    padded = jnp.pad(signal, ((rim_len, 0), (0, 0)))

    def add_tap(tap_index, summed):
        window = lax.dynamic_slice_in_dim(padded, rim_len - tap_index, SEQ, 0)
        return summed + filter_taps[tap_index][None, :] * window

    return lax.fori_loop(0, FILT, add_tap, jnp.zeros((SEQ, CHANNELS), jnp.float32))


def to_half(array):
    return lax.optimization_barrier(array.astype(jnp.bfloat16)).astype(jnp.float32)


def sequence_grads(query, keyrow, gate, values, grad_out, doc_start, filter_taps):
    highest = lax.Precision.HIGHEST
    score_scale = HEAD_DIM ** -0.5
    rim_len = FILT - 1
    signal = values.astype(jnp.float32)
    mixed = causal_filter(signal, filter_taps)
    gate_f32 = gate.astype(jnp.float32)
    hyena_out = (gate_f32 * mixed).astype(jnp.bfloat16)
    positions = jnp.arange(SEQ, dtype=jnp.int32)
    allowed = (positions[None, :] <= positions[:, None]) & (positions[None, :] >= doc_start[:, None])

    def split_heads(array):
        return array.reshape(SEQ, HEADS, HEAD_DIM).transpose(1, 0, 2)

    def head_grads(packed):
        query_f32 = packed[0].astype(jnp.float32)
        key_f32 = packed[1].astype(jnp.float32)
        hyena_f32 = packed[2].astype(jnp.float32)
        grad_f32 = packed[3].astype(jnp.float32)
        scores = jnp.dot(query_f32, key_f32.T, precision=highest, preferred_element_type=jnp.float32) * score_scale
        masked = jnp.where(allowed, scores, -jnp.inf)
        row_top = jnp.max(masked, -1, keepdims=True)
        weights = jnp.where(allowed, jnp.exp(masked - row_top), 0.0)
        probs = weights / jnp.sum(weights, -1, keepdims=True)
        probs_half = to_half(probs)
        attended = jnp.dot(probs_half, hyena_f32, precision=highest, preferred_element_type=jnp.float32)
        deltas = jnp.sum(grad_f32 * attended, -1)
        dprob = jnp.dot(grad_f32, hyena_f32.T, precision=highest, preferred_element_type=jnp.float32)
        dscore = to_half(probs * (dprob - deltas[:, None]))
        grad_query = jnp.dot(dscore, key_f32, precision=highest, preferred_element_type=jnp.float32) * score_scale
        grad_key = jnp.dot(dscore.T, query_f32, precision=highest, preferred_element_type=jnp.float32) * score_scale
        grad_hyena = jnp.dot(probs_half.T, grad_f32, precision=highest, preferred_element_type=jnp.float32)
        return grad_query, grad_key, grad_hyena

    head_results = lax.map(head_grads, (split_heads(query), split_heads(keyrow), split_heads(hyena_out), split_heads(grad_out)))

    def join_heads(array):
        return array.transpose(1, 0, 2).reshape(SEQ, CHANNELS)

    grad_query = join_heads(head_results[0])
    grad_key = join_heads(head_results[1])
    grad_hyena = join_heads(head_results[2])
    grad_gate = (grad_hyena * mixed).astype(jnp.bfloat16)
    grad_mixed = (grad_hyena * gate_f32).astype(jnp.bfloat16).astype(jnp.float32)
    grad_padded = jnp.pad(grad_mixed, ((0, rim_len), (0, 0)))

    def add_back(tap_index, summed):
        window = lax.dynamic_slice_in_dim(grad_padded, tap_index, SEQ, 0)
        return summed + filter_taps[tap_index][None, :] * window

    grad_values = lax.fori_loop(0, FILT, add_back, jnp.zeros((SEQ, CHANNELS), jnp.float32))
    value_padded = jnp.pad(signal, ((rim_len, 0), (0, 0)))

    def tap_sum(tap_index):
        window = lax.dynamic_slice_in_dim(value_padded, rim_len - tap_index, SEQ, 0)
        return jnp.sum(grad_mixed * window, 0)

    grad_filter = lax.map(tap_sum, jnp.arange(FILT, dtype=jnp.int32))
    return (grad_query.astype(jnp.bfloat16), grad_key.astype(jnp.bfloat16),
            grad_gate, grad_values.astype(jnp.bfloat16), grad_filter)


def reference(queries, keys, gate, values, grad_out, doc_start, filter_taps):
    def one_sequence(packed):
        return sequence_grads(packed[0], packed[1], packed[2], packed[3], packed[4], packed[5], filter_taps)

    results = lax.map(one_sequence, (queries, keys, gate, values, grad_out, doc_start))
    return results[0], results[1], results[2], results[3], jnp.sum(results[4], 0)
```

```python
import functools

import jax
import jax.numpy as jnp
from jax import lax
from jax.experimental import pallas as pl
from jax.experimental.pallas import tpu as pltpu
from jax.sharding import PartitionSpec as P

HEADS = 32
HEAD_DIM = 128
LONGEST_DOC = 640
LANES = 128
QUERY_ROWS = 256

f32 = jnp.float32
bf16 = jnp.bfloat16
contract_last = (((1,), (1,)), ((), ()))
contract_first = (((0,), (0,)), ((), ()))


def rows_at(start, size):
    return pl.ds(pl.multiple_of(start, LANES), size)


def mix_forward(seq_blocks, values, gate, taps, taken, turned, mixed, hyena):
    blocks = values.shape[0] // LANES

    @pl.loop(0, blocks)
    def _(n):
        piece = values[rows_at(n * LANES, LANES), :].astype(f32)
        taken[pl.ds(n, LANES, stride=blocks), :] = piece.T

    row = lax.broadcasted_iota(jnp.int32, (LANES, LANES), 0)
    col = lax.broadcasted_iota(jnp.int32, (LANES, LANES), 1)
    block_row = lax.broadcasted_iota(jnp.int32, (blocks, LANES), 0)
    first = lax.rem(block_row, seq_blocks) == 0

    def channel(c, carry):
        own = taken[pl.ds(pl.multiple_of(c * blocks, blocks), blocks), :]
        before = jnp.where(first, 0.0, pltpu.roll(own, 1, 0))
        both = jnp.concatenate([own, before], 1).astype(bf16)
        circle = jnp.broadcast_to(taps[pl.ds(c, 1), :], (LANES, LANES))
        circle = pltpu.roll(circle, 0, 1, stride=1, stride_axis=0)
        near = jnp.where(row <= col, circle, 0.0).astype(bf16)
        far = jnp.where(row > col, circle, 0.0).astype(bf16)
        turned[pl.ds(pl.multiple_of(c * blocks, blocks), blocks), :] = jnp.dot(
            both, jnp.concatenate([near, far], 0), preferred_element_type=f32
        )
        return carry

    lax.fori_loop(0, LANES, channel, 0, unroll=4)

    @pl.loop(0, blocks)
    def _(n):
        at = rows_at(n * LANES, LANES)
        piece = turned[pl.ds(n, LANES, stride=blocks), :].T
        mixed[at, :] = piece
        hyena[at, :] = (gate[at, :].astype(f32) * piece).astype(bf16)


def attend(seq_rows, queries, keys, grad_out, starts, hyena, grad_queries, acc_keys, acc_hyena):
    scale = HEAD_DIM ** (-0.5)
    acc_keys[...] = jnp.zeros_like(acc_keys)
    acc_hyena[...] = jnp.zeros_like(acc_hyena)

    def query_block(base, q_first, k_first, width):
        q_at = rows_at(base + q_first, QUERY_ROWS)
        k_at = rows_at(base + k_first, width)
        q = queries[q_at, :]
        g = grad_out[q_at, :]
        k = keys[k_at, :]
        h = hyena[k_at, :]
        key_pos = k_first + lax.broadcasted_iota(jnp.int32, (QUERY_ROWS, width), 1)
        query_pos = q_first + lax.broadcasted_iota(jnp.int32, (QUERY_ROWS, width), 0)
        allowed = (key_pos <= query_pos) & (key_pos >= starts[q_at, :])
        scores = lax.dot_general(q, k, contract_last, preferred_element_type=f32) * scale
        scores = jnp.where(allowed, scores, -1e30)
        weights = jnp.exp(scores - jnp.max(scores, 1, keepdims=True))
        probs = weights * (1.0 / jnp.sum(weights, 1, keepdims=True))
        half = probs.astype(bf16)
        dprob = lax.dot_general(g, h, contract_last, preferred_element_type=f32)
        delta = jnp.sum(half.astype(f32) * dprob, 1, keepdims=True)
        dscore = (probs * (dprob - delta)).astype(bf16)
        grad_queries[q_at, :] = (jnp.dot(dscore, k, preferred_element_type=f32) * scale).astype(bf16)
        acc_keys[k_at, :] += lax.dot_general(dscore, q, contract_first, preferred_element_type=f32)
        acc_hyena[k_at, :] += lax.dot_general(half, g, contract_first, preferred_element_type=f32)

    full = QUERY_ROWS + LONGEST_DOC
    short = min(seq_rows // QUERY_ROWS, -(-LONGEST_DOC // QUERY_ROWS))

    @pl.loop(0, queries.shape[0] // seq_rows)
    def _(b):
        base = b * seq_rows
        for n in range(short):
            query_block(base, n * QUERY_ROWS, 0, (n + 1) * QUERY_ROWS)

        @pl.loop(short, seq_rows // QUERY_ROWS)
        def _(n):
            query_block(base, n * QUERY_ROWS, n * QUERY_ROWS - LONGEST_DOC, full)


def mix_backward(
    seq_blocks, gate, values, back_taps, taken, turned, mixed, acc_keys, acc_hyena,
    grad_keys, grad_gate, grad_values, grad_filter, given,
):
    scale = HEAD_DIM ** (-0.5)
    blocks = gate.shape[0] // LANES
    row = lax.broadcasted_iota(jnp.int32, (LANES, LANES), 0)
    col = lax.broadcasted_iota(jnp.int32, (LANES, LANES), 1)
    flip = jnp.where(row + col == LANES - 1, 1.0, 0.0).astype(bf16)

    @pl.loop(0, blocks)
    def _(n):
        at = rows_at(n * LANES, LANES)
        grad = acc_hyena[at, :]
        grad_keys[at, :] = (acc_keys[at, :] * scale).astype(bf16)
        grad_gate[at, :] = (grad * mixed[at, :]).astype(bf16)
        grad_mixed = (grad * gate[at, :].astype(f32)).astype(bf16).astype(f32)
        given[pl.ds(n, LANES, stride=blocks), :] = grad_mixed.T
        taken[pl.ds(n, LANES, stride=blocks), :] = lax.dot_general(
            values[at, :], flip, contract_first, preferred_element_type=f32
        )

    block_row = lax.broadcasted_iota(jnp.int32, (blocks, LANES), 0)
    first = lax.rem(block_row, seq_blocks) == 0
    last = lax.rem(block_row, seq_blocks) == seq_blocks - 1

    def channel(c, carry):
        at = pl.ds(pl.multiple_of(c * blocks, blocks), blocks)
        grad = given[at, :]
        after = jnp.where(last, 0.0, pltpu.roll(grad, blocks - 1, 0))
        grads = jnp.concatenate([grad, after], 1).astype(bf16)
        circle = jnp.broadcast_to(back_taps[pl.ds(c, 1), :], (LANES, LANES))
        circle = pltpu.roll(circle, 0, 1, stride=1, stride_axis=0)
        near = jnp.where(row >= col, circle, 0.0).astype(bf16)
        far = jnp.where(row < col, circle, 0.0).astype(bf16)
        turned[at, :] = jnp.dot(grads, jnp.concatenate([near, far], 0), preferred_element_type=f32)
        own = taken[at, :]
        before = jnp.where(first, 0.0, pltpu.roll(own, 1, 0))
        both = jnp.concatenate([own, before], 1).astype(bf16)
        pairs = lax.dot_general(both, grad.astype(bf16), contract_first, preferred_element_type=f32)
        by_lag = jnp.where(row + col >= LANES - 1, pairs[:LANES], pairs[LANES:])
        by_lag = pltpu.roll(by_lag, 1, 1, stride=1, stride_axis=0)
        grad_filter[pl.ds(c, 1), :] = jnp.sum(by_lag, 0, keepdims=True)
        return carry

    lax.fori_loop(0, LANES, channel, 0, unroll=4)

    @pl.loop(0, blocks)
    def _(n):
        piece = turned[pl.ds(n, LANES, stride=blocks), :].T
        grad_values[rows_at(n * LANES, LANES), :] = piece.astype(bf16)


def head_kernel(
    seq_rows, queries, keys, gate, values, grad_out, starts, taps, back_taps,
    grad_queries, grad_keys, grad_gate, grad_values, grad_filter,
    taken, given, turned, mixed, hyena, acc_keys, acc_hyena,
):
    seq_blocks = seq_rows // LANES
    mix_forward(seq_blocks, values, gate, taps, taken, turned, mixed, hyena)
    attend(seq_rows, queries, keys, grad_out, starts, hyena, grad_queries, acc_keys, acc_hyena)
    mix_backward(
        seq_blocks, gate, values, back_taps, taken, turned, mixed, acc_keys, acc_hyena,
        grad_keys, grad_gate, grad_values, grad_filter, given,
    )


def head_grads(seq_rows, queries, keys, gate, values, grad_out, starts, taps):
    rows = queries.shape[0]
    half = jax.ShapeDtypeStruct((rows, LANES), bf16)
    taps = taps.T
    back_taps = jnp.roll(taps[:, ::-1], 1, 1)
    vmem = pl.BlockSpec(memory_space=pltpu.VMEM)
    *grads, grad_filter = pl.pallas_call(
        functools.partial(head_kernel, seq_rows),
        out_shape=[half] * 4 + [jax.ShapeDtypeStruct((LANES, LANES), f32)],
        in_specs=[vmem] * 8,
        out_specs=[vmem] * 5,
        scratch_shapes=[pltpu.VMEM((rows, LANES), f32)] * 4
        + [pltpu.VMEM((rows, LANES), bf16)]
        + [pltpu.VMEM((rows, LANES), f32)] * 2,
        compiler_params=pltpu.CompilerParams(vmem_limit_bytes=48 * 2**20),
    )(queries, keys, gate, values, grad_out, starts.reshape(rows, 1), taps, back_taps)
    return grads, grad_filter.T


def on_device(queries, keys, gate, values, grad_out, doc_start, filter_taps, *, axes, parts):
    tok_rows, channels = queries.shape[1:]
    wide = channels // parts
    seq_rows = lax.axis_size("ctx") * tok_rows

    def to_heads(x):
        x = x[0].reshape(tok_rows, parts, wide).transpose(1, 0, 2)
        return lax.all_to_all(x, axes, 0, 0).reshape(-1, wide)

    def to_rows(x):
        x = lax.all_to_all(x.reshape(parts, tok_rows, wide), axes, 0, 0)
        return x.transpose(1, 0, 2).reshape(1, tok_rows, channels)

    starts = lax.all_gather(doc_start[0], axes, tiled=True)
    own_taps = lax.dynamic_slice_in_dim(filter_taps, lax.axis_index(axes) * wide, wide, 1)
    arrived = [to_heads(x) for x in (queries, keys, gate, values, grad_out)]
    heads = []
    for at in range(0, wide, LANES):
        heads.append(head_grads(
            seq_rows, *(x[:, at : at + LANES] for x in arrived), starts, own_taps[:, at : at + LANES]
        ))
    grads = [jnp.concatenate(pieces, 1) for pieces in zip(*(h[0] for h in heads))]
    own_filter = jnp.concatenate([h[1] for h in heads], 1)
    if "dp" not in axes:
        own_filter = lax.psum(own_filter, "dp")
    grad_filter = lax.all_gather(own_filter, axes, axis=1, tiled=True)
    return (*(to_rows(x) for x in grads), grad_filter)


def solution(mesh):
    axes = ("dp", "ctx")
    if HEADS % (mesh.shape["dp"] * mesh.shape["ctx"]):
        axes = ("ctx",)
    parts = 1
    for axis in axes:
        parts *= mesh.shape[axis]
    rows = P("dp", "ctx", None)
    return jax.shard_map(
        functools.partial(on_device, axes=axes, parts=parts),
        mesh=mesh,
        in_specs=(rows, rows, rows, rows, rows, P("dp", "ctx"), P()),
        out_specs=(rows, rows, rows, rows, P()),
        check_vma=False,
    )
```

```python
import functools

import jax
import jax.numpy as jnp
from jax import lax
from jax.experimental import pallas as pl
from jax.experimental.pallas import tpu as pltpu
from jax.sharding import PartitionSpec as P

HEADS = 32
HEAD_DIM = 128
LONGEST_DOC = 640
LANES = 128
QUERY_ROWS = 256

f32 = jnp.float32
bf16 = jnp.bfloat16
contract_last = (((1,), (1,)), ((), ()))
contract_first = (((0,), (0,)), ((), ()))


def rows_at(start, size):
    return pl.ds(pl.multiple_of(start, LANES), size)


def mix_forward(seq_blocks, wait_for, values, gate, taps, taken, turned, mixed, hyena):
    blocks = values.shape[0] // LANES
    wait_for(0)

    @pl.loop(0, blocks)
    def _(n):
        piece = values[rows_at(n * LANES, LANES), :].astype(f32)
        taken[pl.ds(n, LANES, stride=blocks), :] = piece.T

    row = lax.broadcasted_iota(jnp.int32, (LANES, LANES), 0)
    col = lax.broadcasted_iota(jnp.int32, (LANES, LANES), 1)
    block_row = lax.broadcasted_iota(jnp.int32, (blocks, LANES), 0)
    first = lax.rem(block_row, seq_blocks) == 0

    def channel(c, carry):
        own = taken[pl.ds(pl.multiple_of(c * blocks, blocks), blocks), :]
        before = jnp.where(first, 0.0, pltpu.roll(own, 1, 0))
        both = jnp.concatenate([own, before], 1).astype(bf16)
        circle = jnp.broadcast_to(taps[pl.ds(c, 1), :], (LANES, LANES))
        circle = pltpu.roll(circle, 0, 1, stride=1, stride_axis=0)
        near = jnp.where(row <= col, circle, 0.0).astype(bf16)
        far = jnp.where(row > col, circle, 0.0).astype(bf16)
        turned[pl.ds(pl.multiple_of(c * blocks, blocks), blocks), :] = jnp.dot(
            both, jnp.concatenate([near, far], 0), preferred_element_type=f32
        )
        return carry

    lax.fori_loop(0, LANES, channel, 0, unroll=4)
    flip = jnp.where(row + col == LANES - 1, 1.0, 0.0).astype(bf16)
    wait_for(1)

    @pl.loop(0, blocks)
    def _(n):
        at = rows_at(n * LANES, LANES)
        taken[pl.ds(n, LANES, stride=blocks), :] = lax.dot_general(
            values[at, :], flip, contract_first, preferred_element_type=f32
        )
        piece = turned[pl.ds(n, LANES, stride=blocks), :].T
        mixed[at, :] = piece
        hyena[at, :] = (gate[at, :].astype(f32) * piece).astype(bf16)


def attend(
    seq_rows, turn, finish, queries, keys, grad_out, starts, hyena, grad_queries, acc_keys, acc_hyena
):
    scale = HEAD_DIM ** (-0.5)
    acc_keys[...] = jnp.zeros_like(acc_keys)
    acc_hyena[...] = jnp.zeros_like(acc_hyena)
    sequences = queries.shape[0] // seq_rows

    def query_block(base, q_first, k_first, width):
        q_at = rows_at(base + q_first, QUERY_ROWS)
        k_at = rows_at(base + k_first, width)
        q = queries[q_at, :]
        g = grad_out[q_at, :]
        k = keys[k_at, :]
        h = hyena[k_at, :]
        key_pos = k_first + lax.broadcasted_iota(jnp.int32, (QUERY_ROWS, width), 1)
        query_pos = q_first + lax.broadcasted_iota(jnp.int32, (QUERY_ROWS, width), 0)
        allowed = (key_pos <= query_pos) & (key_pos >= starts[q_at, :])
        scores = lax.dot_general(q, k, contract_last, preferred_element_type=f32) * scale
        scores = jnp.where(allowed, scores, -1e30)
        weights = jnp.exp(scores - jnp.max(scores, 1, keepdims=True))
        probs = weights * (1.0 / jnp.sum(weights, 1, keepdims=True))
        half = probs.astype(bf16)
        dprob = lax.dot_general(g, h, contract_last, preferred_element_type=f32)
        delta = jnp.sum(half.astype(f32) * dprob, 1, keepdims=True)
        dscore = (probs * (dprob - delta)).astype(bf16)
        grad_queries[q_at, :] = (jnp.dot(dscore, k, preferred_element_type=f32) * scale).astype(bf16)
        acc_keys[k_at, :] += lax.dot_general(dscore, q, contract_first, preferred_element_type=f32)
        acc_hyena[k_at, :] += lax.dot_general(half, g, contract_first, preferred_element_type=f32)

    full = QUERY_ROWS + LONGEST_DOC
    short = min(seq_rows // QUERY_ROWS, -(-LONGEST_DOC // QUERY_ROWS))

    @pl.loop(0, sequences)
    def _(step):
        b = lax.rem(step + turn, sequences)
        base = b * seq_rows
        for n in range(short):
            query_block(base, n * QUERY_ROWS, 0, (n + 1) * QUERY_ROWS)

        @pl.loop(short, seq_rows // QUERY_ROWS)
        def _(n):
            query_block(base, n * QUERY_ROWS, n * QUERY_ROWS - LONGEST_DOC, full)

        finish(b)


def finish_sequence(
    b, seq_blocks, gate, mixed, acc_keys, acc_hyena, grad_keys, grad_gate, given
):
    scale = HEAD_DIM ** (-0.5)
    blocks = gate.shape[0] // LANES

    @pl.loop(0, seq_blocks)
    def _(step):
        n = b * seq_blocks + step
        at = rows_at(n * LANES, LANES)
        grad = acc_hyena[at, :]
        grad_keys[at, :] = (acc_keys[at, :] * scale).astype(bf16)
        grad_gate[at, :] = (grad * mixed[at, :]).astype(bf16)
        grad_mixed = (grad * gate[at, :].astype(f32)).astype(bf16).astype(f32)
        given[pl.ds(n, LANES, stride=blocks), :] = grad_mixed.T


def mix_backward(seq_blocks, back_taps, taken, given, turned, grad_values, by_channel):
    blocks = given.shape[0] // LANES
    row = lax.broadcasted_iota(jnp.int32, (LANES, LANES), 0)
    col = lax.broadcasted_iota(jnp.int32, (LANES, LANES), 1)
    block_row = lax.broadcasted_iota(jnp.int32, (blocks, LANES), 0)
    first = lax.rem(block_row, seq_blocks) == 0
    last = lax.rem(block_row, seq_blocks) == seq_blocks - 1

    def channel(c, carry):
        at = pl.ds(pl.multiple_of(c * blocks, blocks), blocks)
        grad = given[at, :]
        after = jnp.where(last, 0.0, pltpu.roll(grad, blocks - 1, 0))
        grads = jnp.concatenate([grad, after], 1).astype(bf16)
        circle = jnp.broadcast_to(back_taps[pl.ds(c, 1), :], (LANES, LANES))
        circle = pltpu.roll(circle, 0, 1, stride=1, stride_axis=0)
        near = jnp.where(row >= col, circle, 0.0).astype(bf16)
        far = jnp.where(row < col, circle, 0.0).astype(bf16)
        turned[at, :] = jnp.dot(grads, jnp.concatenate([near, far], 0), preferred_element_type=f32)
        own = taken[at, :]
        before = jnp.where(first, 0.0, pltpu.roll(own, 1, 0))
        both = jnp.concatenate([own, before], 1).astype(bf16)
        pairs = lax.dot_general(both, grad.astype(bf16), contract_first, preferred_element_type=f32)
        by_lag = jnp.where(row + col >= LANES - 1, pairs[:LANES], pairs[LANES:])
        by_lag = pltpu.roll(by_lag, 1, 1, stride=1, stride_axis=0)
        by_channel[pl.ds(c, 1), :] = jnp.sum(by_lag, 0, keepdims=True)
        return carry

    lax.fori_loop(0, LANES, channel, 0, unroll=4)

    @pl.loop(0, blocks)
    def _(n):
        piece = turned[pl.ds(n, LANES, stride=blocks), :].T
        grad_values[rows_at(n * LANES, LANES), :] = piece.astype(bf16)


def head_kernel(
    axes, queries, keys, gate, values, grad_out, starts, taps, back_taps,
    to_queries, to_keys, to_gate, to_values, to_filter,
    arrived, starts_in, starts_col, taken, given, turned, mixed, hyena, acc_keys, acc_hyena,
    grad_queries, grad_keys, grad_gate, grad_values, by_channel, grad_filter,
    in_sent, in_got, out_sent, out_got,
):
    tok_rows = queries.shape[0]
    per_seq = lax.axis_size("ctx")
    parts = per_seq * (lax.axis_size("dp") if "dp" in axes else 1)
    seq_rows = per_seq * tok_rows
    seq_blocks = seq_rows // LANES
    me, turn = lax.axis_index("ctx"), 0
    if "dp" in axes:
        turn = lax.axis_index("dp")
        me = turn * per_seq + me

    def device(peer):
        if "dp" in axes:
            return {"dp": lax.div(peer, per_seq), "ctx": lax.rem(peer, per_seq)}
        return {"ctx": peer}

    def others(act):
        @pl.loop(1, parts)
        def _(step):
            act(lax.rem(me + step, parts))

    def send(source, target, sent, got, peer):
        pltpu.make_async_remote_copy(
            src_ref=source, dst_ref=target, send_sem=sent, recv_sem=got,
            device_id=device(peer), device_id_type=pl.DeviceIdType.MESH,
        ).start()

    def lanes_of(part):
        return pl.ds(pl.multiple_of(part * LANES, LANES), LANES)

    def rows_of(part):
        return rows_at(part * tok_rows, tok_rows)

    barrier = pltpu.get_barrier_semaphore()
    others(lambda peer: pl.semaphore_signal(
        barrier, inc=1, device_id=device(peer), device_id_type=pl.DeviceIdType.MESH
    ))
    pl.semaphore_wait(barrier, parts - 1)

    incoming = (values, gate, keys, queries, grad_out)
    for at, source in enumerate(incoming):
        landing = arrived.at[at, rows_of(me)]
        others(lambda peer: send(
            source.at[:, lanes_of(peer)], landing, in_sent.at[at], in_got.at[at], peer
        ))
        pltpu.make_async_copy(source.at[:, lanes_of(me)], landing, in_got.at[at]).start()
        if at == 1:
            others(lambda peer: send(starts, starts_in.at[me], in_sent.at[5], in_got.at[5], peer))
            pltpu.make_async_copy(starts, starts_in.at[me], in_got.at[5]).start()

    def wait_for(at):
        whole = starts_in if at == 5 else arrived.at[at]
        pltpu.make_async_copy(whole, whole, in_got.at[at]).wait()

    v, gates, k, q, g = (arrived.at[at] for at in range(5))
    mix_forward(seq_blocks, wait_for, v, gates, taps, taken, turned, mixed, hyena)
    wait_for(5)

    @pl.loop(0, parts)
    def _(part):
        line = starts_in[part].astype(f32)[:1]
        turned_line = jnp.broadcast_to(line, (LANES, LANES)).T
        starts_col[rows_at(part * LANES, LANES), :] = turned_line[:, :1].astype(jnp.int32)

    for at in (2, 3, 4):
        wait_for(at)

    results = ((grad_queries, to_queries), (grad_keys, to_keys), (grad_gate, to_gate))

    def give(at, source, target, peer):
        @pl.when(peer != me)
        def _():
            send(source, target, out_sent.at[at], out_got.at[at], peer)

        @pl.when(peer == me)
        def _():
            pltpu.make_async_copy(source, target, out_got.at[at]).start()

    def finish(b):
        finish_sequence(
            b, seq_blocks, gates, mixed, acc_keys, acc_hyena, grad_keys, grad_gate, given
        )
        for at, (source, target) in enumerate(results):
            @pl.loop(0, per_seq)
            def _(step):
                peer = b * per_seq + lax.rem(step + lax.axis_index("ctx"), per_seq)
                give(at, source.at[rows_of(peer)], target.at[:, lanes_of(me)], peer)

    attend(
        seq_rows, turn, finish, q, k, g, starts_col, hyena, grad_queries, acc_keys, acc_hyena
    )
    mix_backward(seq_blocks, back_taps, taken, given, turned, grad_values, by_channel)
    grad_filter[...] = by_channel[...].T.astype(bf16)
    own_lanes = lanes_of(me)
    others(lambda peer: send(
        grad_values.at[rows_of(peer)], to_values.at[:, own_lanes], out_sent.at[3], out_got.at[3], peer
    ))
    pltpu.make_async_copy(
        grad_values.at[rows_of(me)], to_values.at[:, own_lanes], out_got.at[3]
    ).start()
    others(lambda peer: send(
        grad_filter, to_filter.at[:, own_lanes], out_sent.at[4], out_got.at[4], peer
    ))
    pltpu.make_async_copy(grad_filter, to_filter.at[:, own_lanes], out_got.at[4]).start()

    remote = pl.ds(0, (parts - 1) * LANES)
    for at in range(5):
        sent = incoming[at].at[:, remote]
        pltpu.make_async_copy(sent, sent, in_sent.at[at]).wait()
    sent = starts_in.at[pl.ds(0, parts - 1)]
    pltpu.make_async_copy(sent, sent, in_sent.at[5]).wait()
    for at, target in enumerate((to_queries, to_keys, to_gate, to_values, to_filter)):
        pltpu.make_async_copy(target, target, out_got.at[at]).wait()
        sent = target.at[:, remote]
        pltpu.make_async_copy(sent, sent, out_sent.at[at]).wait()


def on_device(queries, keys, gate, values, grad_out, doc_start, filter_taps, *, axes, parts):
    tok_rows, channels = queries.shape[1:]
    rows = parts * tok_rows
    own_taps = lax.dynamic_slice_in_dim(filter_taps, lax.axis_index(axes) * LANES, LANES, 1).T
    back_taps = jnp.roll(own_taps[:, ::-1], 1, 1)
    starts = jnp.broadcast_to(doc_start, (8, tok_rows))
    vmem = pl.BlockSpec(memory_space=pltpu.VMEM)
    anywhere = pl.BlockSpec(memory_space=pl.ANY)
    wide = pltpu.VMEM((rows, LANES), f32)
    narrow = pltpu.VMEM((rows, LANES), bf16)
    *grads, grad_filter = pl.pallas_call(
        functools.partial(head_kernel, axes),
        out_shape=[jax.ShapeDtypeStruct((tok_rows, channels), bf16)] * 4
        + [jax.ShapeDtypeStruct(filter_taps.shape, bf16)],
        in_specs=[anywhere] * 5 + [vmem] * 3,
        out_specs=[anywhere] * 5,
        scratch_shapes=[
            pltpu.VMEM((5, rows, LANES), bf16),
            pltpu.VMEM((parts, 8, tok_rows), jnp.int32),
            pltpu.VMEM((rows, 1), jnp.int32),
            wide, wide, wide, wide, narrow, wide, wide,
            narrow, narrow, narrow, narrow,
            pltpu.VMEM((LANES, LANES), f32),
            pltpu.VMEM((LANES, LANES), bf16),
            pltpu.SemaphoreType.DMA((6,)),
            pltpu.SemaphoreType.DMA((6,)),
            pltpu.SemaphoreType.DMA((5,)),
            pltpu.SemaphoreType.DMA((5,)),
        ],
        compiler_params=pltpu.CompilerParams(
            collective_id=0, has_side_effects=True, vmem_limit_bytes=48 * 2**20
        ),
    )(queries[0], keys[0], gate[0], values[0], grad_out[0], starts, own_taps, back_taps)
    grad_filter = grad_filter.astype(f32)
    if "dp" not in axes:
        grad_filter = lax.psum(grad_filter, "dp")
    return (*(x[None] for x in grads), grad_filter)


def solution(mesh):
    axes = ("dp", "ctx")
    if HEADS % (mesh.shape["dp"] * mesh.shape["ctx"]):
        axes = ("ctx",)
    parts = 1
    for axis in axes:
        parts *= mesh.shape[axis]
    rows = P("dp", "ctx", None)
    return jax.shard_map(
        functools.partial(on_device, axes=axes, parts=parts),
        mesh=mesh,
        in_specs=(rows, rows, rows, rows, rows, P("dp", "ctx"), P()),
        out_specs=(rows, rows, rows, rows, P()),
        check_vma=False,
    )
```

```python
import functools

import jax
import jax.numpy as jnp
from jax import lax
from jax.experimental import pallas as pl
from jax.experimental.pallas import tpu as pltpu
from jax.sharding import PartitionSpec as P

HEADS = 32
HEAD_DIM = 128
LONGEST_DOC = 640
LANES = 128
QUERY_ROWS = 256

f32 = jnp.float32
bf16 = jnp.bfloat16
contract_last = (((1,), (1,)), ((), ()))
contract_first = (((0,), (0,)), ((), ()))


def rows_at(start, size):
    return pl.ds(pl.multiple_of(start, LANES), size)


def mix_forward(seq_blocks, wait_for, values, gate, taps, taken, turned, mixed, hyena):
    blocks = values.shape[0] // LANES
    wait_for(0)

    @pl.loop(0, blocks)
    def _(n):
        piece = values[rows_at(n * LANES, LANES), :].astype(f32)
        taken[pl.ds(n, LANES, stride=blocks), :] = piece.T

    row = lax.broadcasted_iota(jnp.int32, (LANES, LANES), 0)
    col = lax.broadcasted_iota(jnp.int32, (LANES, LANES), 1)
    block_row = lax.broadcasted_iota(jnp.int32, (blocks, LANES), 0)
    first = lax.rem(block_row, seq_blocks) == 0

    def channel(c, carry):
        own = taken[pl.ds(pl.multiple_of(c * blocks, blocks), blocks), :]
        before = jnp.where(first, 0.0, pltpu.roll(own, 1, 0))
        both = jnp.concatenate([own, before], 1).astype(bf16)
        circle = jnp.broadcast_to(taps[pl.ds(c, 1), :], (LANES, LANES))
        circle = pltpu.roll(circle, 0, 1, stride=1, stride_axis=0)
        near = jnp.where(row <= col, circle, 0.0).astype(bf16)
        far = jnp.where(row > col, circle, 0.0).astype(bf16)
        turned[pl.ds(pl.multiple_of(c * blocks, blocks), blocks), :] = jnp.dot(
            both, jnp.concatenate([near, far], 0), preferred_element_type=f32
        )
        return carry

    lax.fori_loop(0, LANES, channel, 0, unroll=4)
    flip = jnp.where(row + col == LANES - 1, 1.0, 0.0).astype(bf16)
    wait_for(1)

    @pl.loop(0, blocks)
    def _(n):
        at = rows_at(n * LANES, LANES)
        taken[pl.ds(n, LANES, stride=blocks), :] = lax.dot_general(
            values[at, :], flip, contract_first, preferred_element_type=f32
        )
        piece = turned[pl.ds(n, LANES, stride=blocks), :].T
        mixed[at, :] = piece
        hyena[at, :] = (gate[at, :].astype(f32) * piece).astype(bf16)


def attend(
    seq_rows, turn, block_done, finish, queries, keys, grad_out, starts, hyena, grad_queries, acc_keys, acc_hyena
):
    scale = HEAD_DIM ** (-0.5)
    sequences = queries.shape[0] // seq_rows

    def query_block(base, q_first, k_first, width):
        q_at = rows_at(base + q_first, QUERY_ROWS)
        k_at = rows_at(base + k_first, width)
        q = queries[q_at, :]
        g = grad_out[q_at, :]
        k = keys[k_at, :]
        h = hyena[k_at, :]
        key_pos = k_first + lax.broadcasted_iota(jnp.int32, (QUERY_ROWS, width), 1)
        query_pos = q_first + lax.broadcasted_iota(jnp.int32, (QUERY_ROWS, width), 0)
        allowed = (key_pos <= query_pos) & (key_pos >= starts[q_at, :])
        scores = lax.dot_general(q, k, contract_last, preferred_element_type=f32) * scale
        scores = jnp.where(allowed, scores, -1e30)
        weights = jnp.exp(scores - jnp.max(scores, 1, keepdims=True))
        probs = weights * (1.0 / jnp.sum(weights, 1, keepdims=True))
        half = probs.astype(bf16)
        dprob = lax.dot_general(g, h, contract_last, preferred_element_type=f32)
        delta = jnp.sum(half.astype(f32) * dprob, 1, keepdims=True)
        dscore = (probs * (dprob - delta)).astype(bf16)
        grad_queries[q_at, :] = (jnp.dot(dscore, k, preferred_element_type=f32) * scale).astype(bf16)
        acc_keys[k_at, :] += lax.dot_general(dscore, q, contract_first, preferred_element_type=f32)
        acc_hyena[k_at, :] += lax.dot_general(half, g, contract_first, preferred_element_type=f32)

    full = QUERY_ROWS + LONGEST_DOC
    short = min(seq_rows // QUERY_ROWS, -(-LONGEST_DOC // QUERY_ROWS))

    @pl.loop(0, sequences)
    def _(step):
        b = lax.rem(step + turn, sequences)
        base = b * seq_rows
        for n in range(short):
            query_block(base, n * QUERY_ROWS, 0, (n + 1) * QUERY_ROWS)
            block_done(base + n * QUERY_ROWS)

        @pl.loop(short, seq_rows // QUERY_ROWS)
        def _(n):
            query_block(base, n * QUERY_ROWS, n * QUERY_ROWS - LONGEST_DOC, full)
            block_done(base + n * QUERY_ROWS)

        finish(b)


def finish_sequence(
    b, seq_blocks, gate, mixed, acc_keys, acc_hyena, grad_keys, grad_gate, given
):
    scale = HEAD_DIM ** (-0.5)
    blocks = gate.shape[0] // LANES

    @pl.loop(0, seq_blocks)
    def _(step):
        n = b * seq_blocks + step
        at = rows_at(n * LANES, LANES)
        grad = acc_hyena[at, :]
        grad_keys[at, :] = (acc_keys[at, :] * scale).astype(bf16)
        grad_gate[at, :] = (grad * mixed[at, :]).astype(bf16)
        grad_mixed = (grad * gate[at, :].astype(f32)).astype(bf16).astype(f32)
        given[pl.ds(n, LANES, stride=blocks), :] = grad_mixed.T


def mix_backward(
    seq_blocks, filter_done, back_taps, taken, given, turned, grad_values, by_channel
):
    blocks = given.shape[0] // LANES
    row = lax.broadcasted_iota(jnp.int32, (LANES, LANES), 0)
    col = lax.broadcasted_iota(jnp.int32, (LANES, LANES), 1)
    block_row = lax.broadcasted_iota(jnp.int32, (blocks, LANES), 0)
    first = lax.rem(block_row, seq_blocks) == 0
    last = lax.rem(block_row, seq_blocks) == seq_blocks - 1

    def pair_channel(c, carry):
        at = pl.ds(pl.multiple_of(c * blocks, blocks), blocks)
        own = taken[at, :]
        before = jnp.where(first, 0.0, pltpu.roll(own, 1, 0))
        both = jnp.concatenate([own, before], 1).astype(bf16)
        pairs = lax.dot_general(
            both, given[at, :].astype(bf16), contract_first, preferred_element_type=f32
        )
        by_lag = jnp.where(row + col >= LANES - 1, pairs[:LANES], pairs[LANES:])
        by_lag = pltpu.roll(by_lag, 1, 1, stride=1, stride_axis=0)
        by_channel[pl.ds(c, 1), :] = jnp.sum(by_lag, 0, keepdims=True)
        return carry

    lax.fori_loop(0, LANES, pair_channel, 0, unroll=4)
    filter_done()

    def channel(c, carry):
        at = pl.ds(pl.multiple_of(c * blocks, blocks), blocks)
        grad = given[at, :]
        after = jnp.where(last, 0.0, pltpu.roll(grad, blocks - 1, 0))
        grads = jnp.concatenate([grad, after], 1).astype(bf16)
        circle = jnp.broadcast_to(back_taps[pl.ds(c, 1), :], (LANES, LANES))
        circle = pltpu.roll(circle, 0, 1, stride=1, stride_axis=0)
        near = jnp.where(row >= col, circle, 0.0).astype(bf16)
        far = jnp.where(row < col, circle, 0.0).astype(bf16)
        turned[at, :] = jnp.dot(grads, jnp.concatenate([near, far], 0), preferred_element_type=f32)
        return carry

    lax.fori_loop(0, LANES, channel, 0, unroll=4)

    @pl.loop(0, blocks)
    def _(n):
        piece = turned[pl.ds(n, LANES, stride=blocks), :].T
        grad_values[rows_at(n * LANES, LANES), :] = piece.astype(bf16)


def head_kernel(
    axes, queries, keys, gate, values, grad_out, starts, all_taps,
    to_queries, to_keys, to_gate, to_values, to_filter,
    arrived, starts_in, starts_col, taken, given, turned, mixed, hyena, acc_keys, acc_hyena,
    grad_queries, grad_keys, grad_gate, grad_values, by_channel, grad_filter,
    near_filter, taps_in, taps, back_taps, in_sent, in_got, out_sent, out_got, taps_got,
):
    tok_rows = queries.shape[0]
    per_seq = lax.axis_size("ctx")
    parts = per_seq * (lax.axis_size("dp") if "dp" in axes else 1)
    seq_rows = per_seq * tok_rows
    seq_blocks = seq_rows // LANES
    me, turn = lax.axis_index("ctx"), 0
    if "dp" in axes:
        turn = lax.axis_index("dp")
        me = turn * per_seq + me

    def device(peer):
        if "dp" in axes:
            return {"dp": lax.div(peer, per_seq), "ctx": lax.rem(peer, per_seq)}
        return {"ctx": peer}

    def others(act):
        @pl.loop(1, parts)
        def _(step):
            act(lax.rem(me + step, parts))

    def send(source, target, sent, got, peer):
        pltpu.make_async_remote_copy(
            src_ref=source, dst_ref=target, send_sem=sent, recv_sem=got,
            device_id=device(peer), device_id_type=pl.DeviceIdType.MESH,
        ).start()

    def lanes_of(part):
        return pl.ds(pl.multiple_of(part * LANES, LANES), LANES)

    def rows_of(part):
        return rows_at(part * tok_rows, tok_rows)

    own_taps = pltpu.make_async_copy(all_taps.at[:, lanes_of(me)], taps_in, taps_got)
    own_taps.start()
    barrier = pltpu.get_barrier_semaphore()
    others(lambda peer: pl.semaphore_signal(
        barrier, inc=1, device_id=device(peer), device_id_type=pl.DeviceIdType.MESH
    ))
    pl.semaphore_wait(barrier, parts - 1)

    incoming = (values, gate, keys, queries, grad_out)
    for at, source in enumerate(incoming):
        landing = arrived.at[at, rows_of(me)]
        others(lambda peer: send(
            source.at[:, lanes_of(peer)], landing, in_sent.at[at], in_got.at[at], peer
        ))
        pltpu.make_async_copy(source.at[:, lanes_of(me)], landing, in_got.at[at]).start()
        if at == 1:
            others(lambda peer: send(starts, starts_in.at[me], in_sent.at[5], in_got.at[5], peer))
            pltpu.make_async_copy(starts, starts_in.at[me], in_got.at[5]).start()

    def wait_for(at):
        whole = starts_in if at == 5 else arrived.at[at]
        pltpu.make_async_copy(whole, whole, in_got.at[at]).wait()

    row = lax.broadcasted_iota(jnp.int32, (LANES, LANES), 0)
    col = lax.broadcasted_iota(jnp.int32, (LANES, LANES), 1)
    own_taps.wait()
    taps[...] = taps_in[...].T
    turn_back = jnp.where(lax.rem(row + col, LANES) == 0, 1.0, 0.0).astype(bf16)
    back_taps[...] = jnp.dot(
        taps[...].astype(bf16), turn_back, preferred_element_type=f32
    )
    v, gates, k, q, g = (arrived.at[at] for at in range(5))
    mix_forward(seq_blocks, wait_for, v, gates, taps, taken, turned, mixed, hyena)
    wait_for(5)

    @pl.loop(0, parts)
    def _(part):
        line = starts_in[part].astype(f32)[:1]
        turned_line = jnp.broadcast_to(line, (LANES, LANES)).T
        starts_col[rows_at(part * LANES, LANES), :] = turned_line[:, :1].astype(jnp.int32)

    acc_keys[...] = jnp.zeros_like(acc_keys)
    acc_hyena[...] = jnp.zeros_like(acc_hyena)
    for at in (2, 3, 4):
        wait_for(at)

    results = ((1, grad_keys, to_keys), (2, grad_gate, to_gate))

    def give(at, source, target, peer):
        @pl.when(peer != me)
        def _():
            send(source, target, out_sent.at[at], out_got.at[at], peer)

        @pl.when(peer == me)
        def _():
            pltpu.make_async_copy(source, target, out_got.at[at]).start()

    def block_done(first_row):
        for part in range(QUERY_ROWS // tok_rows):
            peer = lax.div(first_row, tok_rows) + part
            give(0, grad_queries.at[rows_of(peer)], to_queries.at[:, lanes_of(me)], peer)

    def finish(b):
        finish_sequence(
            b, seq_blocks, gates, mixed, acc_keys, acc_hyena, grad_keys, grad_gate, given
        )
        for at, source, target in results:
            @pl.loop(0, per_seq)
            def _(step):
                peer = b * per_seq + lax.rem(step + lax.axis_index("ctx"), per_seq)
                give(at, source.at[rows_of(peer)], target.at[:, lanes_of(me)], peer)

    attend(
        seq_rows, turn, block_done, finish, q, k, g, starts_col, hyena, grad_queries, acc_keys, acc_hyena
    )
    mine = lax.axis_index("ctx")

    def seq_device(step):
        peer = lax.rem(mine + step, per_seq)
        return turn * per_seq + peer if "dp" in axes else peer

    def filter_done():
        grad_filter[...] = by_channel[...].T.astype(bf16)
        landing = near_filter.at[:, lanes_of(mine)]

        @pl.loop(1, per_seq)
        def _(step):
            send(grad_filter, landing, out_sent.at[4], out_got.at[4], seq_device(step))

        pltpu.make_async_copy(grad_filter, landing, out_got.at[4]).start()

    mix_backward(
        seq_blocks, filter_done, back_taps, taken, given, turned, grad_values, by_channel
    )
    own_lanes = lanes_of(me)

    def give_values(begin, end):
        @pl.loop(begin, end)
        def _(step):
            peer = lax.rem(me + step, parts)
            send(
                grad_values.at[rows_of(peer)], to_values.at[:, own_lanes],
                out_sent.at[3], out_got.at[3], peer,
            )

    give_values(1, parts // 2)
    pltpu.make_async_copy(
        grad_values.at[rows_of(me)], to_values.at[:, own_lanes], out_got.at[3]
    ).start()
    pltpu.make_async_copy(near_filter, near_filter, out_got.at[4]).wait()
    span = per_seq * LANES
    landing = to_filter.at[:, pl.ds(pl.multiple_of(turn * span, LANES), span)]
    for step in range(1, parts // per_seq):
        send(
            near_filter, landing, out_sent.at[5], out_got.at[5],
            lax.rem(me + step * per_seq, parts),
        )
    pltpu.make_async_copy(near_filter, landing, out_got.at[5]).start()
    give_values(parts // 2, parts)

    remote = pl.ds(0, (parts - 1) * LANES)
    for at in range(5):
        sent = incoming[at].at[:, remote]
        pltpu.make_async_copy(sent, sent, in_sent.at[at]).wait()
    sent = starts_in.at[pl.ds(0, parts - 1)]
    pltpu.make_async_copy(sent, sent, in_sent.at[5]).wait()
    for at, target in enumerate((to_queries, to_keys, to_gate, to_values)):
        pltpu.make_async_copy(target, target, out_got.at[at]).wait()
        sent = target.at[:, remote]
        pltpu.make_async_copy(sent, sent, out_sent.at[at]).wait()
    sent = near_filter.at[:, pl.ds(0, span - LANES)]
    pltpu.make_async_copy(sent, sent, out_sent.at[4]).wait()
    pltpu.make_async_copy(to_filter, to_filter, out_got.at[5]).wait()
    if parts > per_seq:
        sent = to_filter.at[:, pl.ds(0, parts * LANES - span)]
        pltpu.make_async_copy(sent, sent, out_sent.at[5]).wait()


def on_device(queries, keys, gate, values, grad_out, doc_start, filter_taps, *, axes, parts):
    tok_rows, channels = queries.shape[1:]
    rows = parts * tok_rows
    starts = jnp.broadcast_to(doc_start, (8, tok_rows))
    vmem = pl.BlockSpec(memory_space=pltpu.VMEM)
    anywhere = pl.BlockSpec(memory_space=pl.ANY)
    wide = pltpu.VMEM((rows, LANES), f32)
    narrow = pltpu.VMEM((rows, LANES), bf16)
    *grads, grad_filter = pl.pallas_call(
        functools.partial(head_kernel, axes),
        out_shape=[jax.ShapeDtypeStruct((tok_rows, channels), bf16)] * 4
        + [jax.ShapeDtypeStruct(filter_taps.shape, bf16)],
        in_specs=[anywhere] * 5 + [vmem, anywhere],
        out_specs=[anywhere] * 5,
        scratch_shapes=[
            pltpu.VMEM((5, rows, LANES), bf16),
            pltpu.VMEM((parts, 8, tok_rows), jnp.int32),
            pltpu.VMEM((rows, 1), jnp.int32),
            wide, wide, wide, wide, narrow, wide, wide,
            narrow, narrow, narrow, narrow,
            pltpu.VMEM((LANES, LANES), f32),
            pltpu.VMEM((LANES, LANES), bf16),
            pltpu.VMEM((LANES, lax.axis_size("ctx") * LANES), bf16),
            pltpu.VMEM((LANES, LANES), f32),
            pltpu.VMEM((LANES, LANES), f32),
            pltpu.VMEM((LANES, LANES), f32),
            pltpu.SemaphoreType.DMA((6,)),
            pltpu.SemaphoreType.DMA((6,)),
            pltpu.SemaphoreType.DMA((6,)),
            pltpu.SemaphoreType.DMA((6,)),
            pltpu.SemaphoreType.DMA,
        ],
        compiler_params=pltpu.CompilerParams(
            collective_id=0, has_side_effects=True, vmem_limit_bytes=48 * 2**20
        ),
    )(queries[0], keys[0], gate[0], values[0], grad_out[0], starts, filter_taps)
    grad_filter = grad_filter.astype(f32)
    if "dp" not in axes:
        grad_filter = lax.psum(grad_filter, "dp")
    return (*(x[None] for x in grads), grad_filter)


def solution(mesh):
    axes = ("dp", "ctx")
    if HEADS % (mesh.shape["dp"] * mesh.shape["ctx"]):
        axes = ("ctx",)
    parts = 1
    for axis in axes:
        parts *= mesh.shape[axis]
    rows = P("dp", "ctx", None)
    return jax.shard_map(
        functools.partial(on_device, axes=axes, parts=parts),
        mesh=mesh,
        in_specs=(rows, rows, rows, rows, rows, P("dp", "ctx"), P()),
        out_specs=(rows, rows, rows, rows, P()),
        check_vma=False,
    )
```
